256 devices in a mesh: dp: 32 (over y, z_lo, core), layer: 8 (over z_hi, x).
Axes of the slice: x: 4, y: 4, z: 8 (z_hi: 2, z_lo: 4; z = z_hi * 4 + z_lo), core: 2. Of those that a mesh axis runs over, the one named last changes fastest.
Arguments:
- hidden: bfloat16 [4096, 8192], P('dp'), may hold values from -0.29882812 to 0.29882812
- w_kv: bfloat16 [8, 8192, 1024], P('layer', 'dp'), may hold values from -0.0625 to 0.0625
- queries: bfloat16 [8, 4096, 4096], P('layer', 'dp'), may hold values from -128 to 128
- keys: bfloat16 [8, 4096, 512], P('layer', 'dp'), may hold values from -6 to 6
- values: bfloat16 [8, 4096, 512], P('layer', 'dp'), may hold values from -6 to 6
- out_grad: bfloat16 [8, 4096, 4096], P('layer', 'dp'), may hold values from -6 to 6
- doc_lengths: int32 [32, 8], P('dp'), may hold values from 1 to 64, 128 in all within a row
Outputs:
- grad_hidden: bfloat16 [4096, 8192], P('dp', 'layer')
- grad_w: bfloat16 [8, 8192, 1024], P('layer', 'dp')
The draws below stay inside these ranges and needn't reach their ends.
Inputs may be any that keep to these rules, and one draw needn't show every extreme that they name: `doc_lengths`: each row sums to 128 and its largest entry is 64.
All inputs are finite; a program needn't handle non-finite values.
Results may differ from the reference program's by a relative error of at most 0.0076.
Values may be sent and summed in bfloat16 or wider, within the bound.
A program may use at most 128 MiB of HBM per device.

```python
import math
import jax
import jax.numpy as jnp
import numpy as np
from jax import lax

D = 8192
HEAD_SIZE = 128
KV_HEAD_COUNT = 4
QUERY_PER_KV = 8
TOK_DEV = 128
DOCS = 8
LATER_LAYERS = 8
TOKEN_TOTAL = 4096
HQD = 4096
KVD = 512
KV2 = 1024
MOST_DOC = 64


def base_keys(key):
    return jax.random.normal(key, (LATER_LAYERS, TOKEN_TOTAL, KV_HEAD_COUNT * HEAD_SIZE), jnp.float32)


def draw_keys(key, part):
    shared_factor = base_keys(key)
    key = jax.random.fold_in(key, 11)
    random_jitter = 0.15 * jax.random.normal(key, (LATER_LAYERS, TOKEN_TOTAL, KV_HEAD_COUNT * HEAD_SIZE), jnp.float32)
    position = jnp.arange(TOKEN_TOTAL)
    before = position % 16 == 4
    shifted = jnp.roll(shared_factor, -1, axis=1) + random_jitter
    final_output = jnp.where(before[None, :, None], shifted, shared_factor)
    return jnp.clip(final_output, -6.0, 6.0).astype(jnp.bfloat16)


def draw_queries(key, part):
    key = jax.random.fold_in(key, 12)
    final_output = jax.random.normal(key, (LATER_LAYERS, TOKEN_TOTAL, KV_HEAD_COUNT * QUERY_PER_KV * HEAD_SIZE), jnp.float32)
    return jnp.clip(final_output, -128.0, 128.0).astype(jnp.bfloat16)


def shard_levels(stream_key, extent, cuts, smallest, top_value):
    def one(dim, blocks):
        heights = jax.random.uniform(jax.random.fold_in(jax.random.fold_in(stream_key, 6), dim), (blocks,), jnp.float32, smallest / len(cuts), top_value / len(cuts))
        return jnp.repeat(jnp.exp(heights), extent[dim] // blocks).reshape((-1,) + (1,) * (len(extent) - dim - 1))

    factor_of = one(*cuts[0])
    for cut in cuts[1:]:
        factor_of = factor_of * one(*cut)
    return factor_of


def length_profile(amount, total, bound, slope):
    weights = [(1 << 20) // math.isqrt(rank ** slope) + 1 for rank in range(2, amount + 1)]
    rest, given = total - bound - (amount - 1), [1] * (amount - 1)
    while rest > 0:
        movable = [i for i in range(amount - 1) if given[i] < bound]
        mass, left = sum([weights[i] for i in movable]), rest
        for i in movable:
            addition = min(bound - given[i], max(1, left * weights[i] // mass), rest)
            given[i] = given[i] + addition
            rest = rest - addition
    return np.array([bound] + given)


def ragged(own_key, number_of, total, bound, lean):
    if number_of == 2:
        one = jax.random.randint(own_key, (), max(1, total - bound), min(bound, total - 1) + 1)
        return jnp.stack([one, total - one])
    tallies = jnp.asarray(length_profile(number_of, total, bound, lean), jnp.int32)
    couples = (number_of - 1) // 2
    donor, sink = tallies[1:1 + 2 * couples:2], tallies[2:2 + 2 * couples:2]
    margin = jnp.minimum(donor - 1, bound - sink)
    passed = jax.random.randint(jax.random.fold_in(own_key, 1), (couples,), 0, 1 << 20) % (margin + 1)
    tallies = tallies.at[1:1 + 2 * couples:2].set(donor - passed).at[2:2 + 2 * couples:2].set(sink + passed)
    return tallies[jax.random.permutation(jax.random.fold_in(own_key, 2), number_of)]


def bell_draw(key, dims, spread, reach, pieces=(), kind=jnp.bfloat16):
    array = spread * jax.random.normal(key, dims, jnp.float32)
    if pieces:
        array = array * shard_levels(key, dims, pieces, -0.22, 0.18)
    return jnp.clip(array, -reach, reach).astype(kind)


def setup_inputs(seed: int = 0) -> dict:
    arg_keys = jax.random.split(jax.random.key(seed), 8)
    hidden = bell_draw(arg_keys[0], (TOKEN_TOTAL, D), 0.05, 0.29882812, ((0, 32),))
    w_kv = bell_draw(arg_keys[1], (LATER_LAYERS, D, KV2), D ** -0.5, 0.0625, ((0, 8), (1, 32)))
    queries = draw_queries(jax.random.fold_in(arg_keys[7], 71), 0)
    keys = draw_keys(jax.random.fold_in(arg_keys[7], 71), 0)
    values = bell_draw(arg_keys[4], (LATER_LAYERS, TOKEN_TOTAL, KVD), 1.0, 6.0, ((0, 8), (1, 32)))
    out_grad = bell_draw(arg_keys[5], (LATER_LAYERS, TOKEN_TOTAL, HQD), 1.0, 6.0, ((0, 8), (1, 32)))
    doc_lengths = jax.vmap(lambda own: ragged(own, DOCS, TOK_DEV, MOST_DOC, 2))(jax.random.split(arg_keys[6], (TOKEN_TOTAL // TOK_DEV))).reshape((TOKEN_TOTAL // TOK_DEV, DOCS)).astype(jnp.int32)
    return dict(hidden=hidden, w_kv=w_kv, queries=queries, keys=keys, values=values, out_grad=out_grad, doc_lengths=doc_lengths)


def attend_back(query_block_tile, key_block_tile, value_block_tile, output_gradient_block, lengths):
    element_count = query_block_tile.shape[0]
    scale = HEAD_SIZE ** -0.5
    head_queries = query_block_tile.astype(jnp.float32).reshape(element_count, KV_HEAD_COUNT, QUERY_PER_KV, HEAD_SIZE)
    head_keys = key_block_tile.astype(jnp.float32).reshape(element_count, KV_HEAD_COUNT, HEAD_SIZE)
    head_values = value_block_tile.astype(jnp.float32).reshape(element_count, KV_HEAD_COUNT, HEAD_SIZE)
    output_gradient_head = output_gradient_block.astype(jnp.float32).reshape(element_count, KV_HEAD_COUNT, QUERY_PER_KV, HEAD_SIZE)
    position = jnp.arange(element_count, dtype=jnp.int32)
    ends = jnp.cumsum(lengths.astype(jnp.int32))
    doc_ids = jnp.sum((position[:, None] >= ends[None, :]).astype(jnp.int32), axis=1)
    allowed = (doc_ids[:, None] == doc_ids[None, :]) & (position[None, :] <= position[:, None])
    scores = jnp.einsum('tkgd,skd->kgts', head_queries, head_keys) * scale
    scores = jnp.where(allowed[None, None], scores, jnp.float32(-1e30))
    top = jnp.max(scores, axis=-1, keepdims=True)
    expo = jnp.exp(scores - top)
    probs = expo / jnp.sum(expo, axis=-1, keepdims=True)
    probs_b = probs.astype(jnp.bfloat16).astype(jnp.float32)
    attn_out = jnp.einsum('kgts,skd->tkgd', probs_b, head_values)
    delta = jnp.transpose(jnp.sum(output_gradient_head * attn_out, axis=-1), (1, 2, 0))
    dprobs = jnp.einsum('tkgd,skd->kgts', output_gradient_head, head_values)
    dscores = probs * (dprobs - delta[..., None])
    dscores_b = dscores.astype(jnp.bfloat16).astype(jnp.float32)
    value_gradient = jnp.einsum('kgts,tkgd->skd', probs_b, output_gradient_head)
    key_gradient = jnp.einsum('kgts,tkgd->skd', dscores_b, head_queries) * scale
    merged_gradient = jnp.concatenate([key_gradient.reshape(element_count, KV_HEAD_COUNT * HEAD_SIZE), value_gradient.reshape(element_count, KV_HEAD_COUNT * HEAD_SIZE)], axis=-1)
    return merged_gradient.astype(jnp.bfloat16)


def reference(hidden, w_kv, queries, keys, values, out_grad, doc_lengths):
    blocks = TOKEN_TOTAL // TOK_DEV
    grad_sum = jnp.zeros((TOKEN_TOTAL, D), jnp.float32)
    weight_grads = []
    for layer in range(LATER_LAYERS):
        stacked = (queries[layer].reshape(blocks, TOK_DEV, -1), keys[layer].reshape(blocks, TOK_DEV, -1),
                   values[layer].reshape(blocks, TOK_DEV, -1), out_grad[layer].reshape(blocks, TOK_DEV, -1),
                   doc_lengths)
        key_value_gradient = lax.map(lambda item: attend_back(item[0], item[1], item[2], item[3], item[4]), stacked)
        key_value_gradient = key_value_gradient.reshape(TOKEN_TOTAL, 2 * KV_HEAD_COUNT * HEAD_SIZE)
        weight_grads.append(jnp.dot(hidden.T, key_value_gradient, preferred_element_type=jnp.float32).astype(jnp.bfloat16))
        grad_sum = grad_sum + jnp.dot(key_value_gradient, w_kv[layer].T, preferred_element_type=jnp.float32)
    return grad_sum.astype(jnp.bfloat16), jnp.stack(weight_grads, axis=0)
```

```python
import jax
import jax.numpy as jnp
from jax import lax
from jax.experimental import pallas as pl
from jax.experimental.pallas import tpu as pltpu
from jax.sharding import PartitionSpec as P

HEAD = 128
GROUPS = 4
PER = 8
TOK = 128
DOCS = 8
KV = 512
KV2 = 1024
SCALE = HEAD ** (-0.5)
MESH = pl.DeviceIdType.MESH
NT = (((1,), (1,)), ((), ()))


def xor(a, b):
    return jnp.bitwise_xor(a, b)


def body(lens, hidden, w, q, k, v, dout, gh, gw,
         hid, hid_t, wb, kvb, st, rs, own, gsend, grecv, fs, fin,
         hz_s, hz_r, hc_s, hc_r, hx_s, hx_r, w_s, w_r, kz_s, kz_r, kf_s, kf_r,
         x_s, x_r, g_s, g_r, f_s, f_r, loc):
    dp, ly = lax.axis_index("dp"), lax.axis_index("layer")
    y, z, c = dp // 8, lax.rem(dp // 2, 4), lax.rem(dp, 2)
    h, x = ly // 4, lax.rem(ly, 4)
    y0, y1, z0, z1, x0, x1 = lax.rem(y, 2), y // 2, lax.rem(z, 2), z // 2, lax.rem(x, 2), x // 2

    def dev(yy, zz, cc, hh, xx):
        return ((yy * 4 + zz) * 2 + cc, hh * 4 + xx)

    def send(src, dst, s, r, to):
        return pltpu.make_async_remote_copy(src_ref=src, dst_ref=dst, send_sem=s, recv_sem=r,
                                            device_id=to, device_id_type=MESH)

    a_own, b_own = xor(x1, y0), xor(x0, z1)
    aligned = x0 == z1
    xt = 2 * x1 + z1

    def last(i, i2, j):
        return dev(y, 2 * x0 + xor(z0, i), xor(c, j), xor(y1, i2), xt)

    sib = dev(y, z, 1 - c, h, x)
    zdev = [None] + [dev(y, xor(z, kk), c, h, x) for kk in (1, 2, 3)]
    zsib = [None] + [dev(y, xor(z, kk), 1 - c, h, x) for kk in (1, 2, 3)]
    xdev = [None] + [dev(y, z, c, h, xor(x, qq)) for qq in (1, 2, 3)]
    ydev = [None] + [dev(xor(y, r), z, c, h, x) for r in (1, 2, 3)]

    barrier = pltpu.get_barrier_semaphore()
    for to in [sib] + zdev[1:] + zsib[1:] + xdev[1:] + ydev[1:]:
        pl.semaphore_signal(barrier, inc=1, device_id=to, device_id_type=MESH)
    for i in range(2):
        for i2 in range(2):
            for j in range(2):
                to = last(i, i2, j)
                if i == 0 and j == 0:
                    me = jnp.logical_and(aligned, xor(y1, i2) == h)

                    @pl.when(jnp.logical_not(me))
                    def _():
                        pl.semaphore_signal(barrier, inc=1, device_id=to, device_id_type=MESH)
                else:
                    pl.semaphore_signal(barrier, inc=1, device_id=to, device_id_type=MESH)

    def columns(p, zz, cc):
        return pl.ds(pl.multiple_of(p * 2048 + zz * 512 + cc * 256, 256), 256)

    local = [pltpu.make_async_copy(w.at[0], wb.at[0], loc.at[0])]
    for r in range(4):
        local.append(pltpu.make_async_copy(hidden.at[:, columns(xor(y, r), z, c)],
                                           hid.at[r, pl.ds(0, TOK)], loc.at[1 + r]))
    for cp in local:
        cp.start()

    pl.semaphore_wait(barrier, 20 + jnp.where(aligned, 0, 1))

    hz = []
    for kk in (1, 2, 3):
        for j in range(2):
            rows = pl.ds(kk * 256 + j * TOK, TOK)
            hz.append(send(hidden.at[:, columns(xor(y, x), xor(z, kk), xor(c, j))],
                           hid.at[x, rows], hz_s.at[kk, j], hz_r.at[kk, j], (zsib if j else zdev)[kk]))
    wc = [send(w.at[0], wb.at[r], w_s.at[r], w_r.at[r], ydev[r]) for r in (1, 3, 2)]
    hc = [send(hidden.at[:, columns(xor(y, r), z, 1 - c)], hid.at[r, pl.ds(TOK, TOK)],
               hc_s.at[r], hc_r.at[r], sib) for r in range(4)]
    for cp in hz + wc + hc:
        cp.start()

    row = lax.broadcasted_iota(jnp.int32, (TOK, TOK), 0)
    col = lax.broadcasted_iota(jnp.int32, (TOK, TOK), 1)
    doc_row, doc_col = jnp.zeros_like(row), jnp.zeros_like(col)
    end = jnp.int32(0)
    for d in range(DOCS):
        end = end + lens[0, d]
        doc_row = doc_row + jnp.where(row >= end, 1, 0)
        doc_col = doc_col + jnp.where(col >= end, 1, 0)
    bias = jnp.where((doc_row == doc_col) & (row <= col), 0.0, 1.0)
    off = jnp.concatenate([bias] * PER, axis=1) > 0.5

    def group(g, _):
        wide = pl.multiple_of(g * PER * HEAD, PER * HEAD)
        narrow = pl.multiple_of(g * HEAD, HEAD)
        qg, og = q[0, :, pl.ds(wide, PER * HEAD)], dout[0, :, pl.ds(wide, PER * HEAD)]
        qs = jnp.concatenate([qg[:, n * HEAD:(n + 1) * HEAD] for n in range(PER)], axis=0)
        os = jnp.concatenate([og[:, n * HEAD:(n + 1) * HEAD] for n in range(PER)], axis=0)
        kg, vg = k[0, :, pl.ds(narrow, HEAD)], v[0, :, pl.ds(narrow, HEAD)]
        s = lax.dot_general(kg, qs, NT, preferred_element_type=jnp.float32) * SCALE
        s = jnp.where(off, jnp.float32(-1e30), s)
        e = jnp.exp(s - jnp.max(s, axis=0, keepdims=True))
        p = e / jnp.sum(e, axis=0, keepdims=True)
        pb = p.astype(jnp.bfloat16)
        dp_ = lax.dot_general(vg, os, NT, preferred_element_type=jnp.float32)
        delta = jnp.sum(pb.astype(jnp.float32) * dp_, axis=0, keepdims=True)
        ds = (p * (dp_ - delta)).astype(jnp.bfloat16)
        dv = jnp.dot(pb, os, preferred_element_type=jnp.float32)
        dk = jnp.dot(ds, qs, preferred_element_type=jnp.float32) * SCALE
        kvb[0:TOK, pl.ds(narrow, HEAD)] = dk.astype(jnp.bfloat16)
        kvb[0:TOK, pl.ds(pl.multiple_of(KV + g * HEAD, HEAD), HEAD)] = dv.astype(jnp.bfloat16)
        return 0

    lax.fori_loop(0, GROUPS, group, 0)

    def kv_rows(kk, j):
        return pl.ds(kk * 256 + j * TOK, TOK)

    kz = {kk: send(kvb.at[kv_rows(0, 0)], kvb.at[kv_rows(kk, 0)], kz_s.at[kk], kz_r.at[kk], zdev[kk])
          for kk in (1, 2, 3)}
    kf = {kk: send(kvb.at[kv_rows(kk, 0)], kvb.at[kv_rows(kk, 1)], kf_s.at[kk], kf_r.at[kk], sib)
          for kk in range(4)}
    kf[0].start()
    for kk in (1, 2, 3):
        kz[kk].start()

    for cp in hz:
        cp.wait_recv()
    rest = pl.ds(256, 768)
    hx = [send(hid.at[x, rest], hid.at[x, rest], hx_s.at[qq], hx_r.at[qq], xdev[qq]) for qq in (1, 3, 2)]
    for cp in hx:
        cp.start()
    for cp in local:
        cp.wait()

    def tile(kk, r):
        t = lax.dot_general(kvb[kk * 256:(kk + 1) * 256], wb[r], NT, preferred_element_type=jnp.float32)
        st[kk, r] = t.astype(jnp.bfloat16)
        to_x = 2 * xor(y0, r % 2) + xor(z1, kk // 2)
        qq = xor(to_x, x)

        @pl.when(qq != 0)
        def _():
            send(st.at[kk, r], rs.at[qq, kk % 2, r // 2], x_s.at[kk, r], x_r.at[qq, kk % 2, r // 2],
                 dev(y, z, c, h, to_x)).start()

    for kk in range(4):
        if kk:
            kz[kk].wait_recv()
            kf[kk].start()
        kf[kk].wait_recv()
        for n, r in enumerate((0, 1, 3, 2)):
            if kk == 0 and n:
                wc[n - 1].wait_recv()
            tile(kk, r)

    for cp in hx + hc:
        cp.wait_recv()
    for r in range(4):
        hid_t[r] = hid[r].T
    gc = []
    for r in (2, 1, 3, 0):
        t = jnp.dot(hid_t[r], kvb[...], preferred_element_type=jnp.float32)
        if r:
            gsend[r - 1] = t.astype(jnp.bfloat16)
            cp = send(gsend.at[r - 1], grecv.at[r - 1], g_s.at[r], g_r.at[r], ydev[r])
            cp.start()
            gc.append(cp)
        else:
            own[...] = t

    for i in range(2):
        for i2 in range(2):
            for qq in (1, 2, 3):
                send(rs.at[qq, i, i2], rs.at[qq, i, i2], x_s.at[0, 0], x_r.at[qq, i, i2], xdev[qq]).wait_recv()
            t = st[2 * b_own + i, a_own + 2 * i2].astype(jnp.float32)
            for qq in (1, 2, 3):
                t = t + rs[qq, i, i2].astype(jnp.float32)
            fs[i, i2] = t.astype(jnp.bfloat16)
            ht = xor(y1, i2)
            g = xor(ht, h)
            for j in range(2):
                src = fs.at[i, i2, pl.ds(j * TOK, TOK)]
                to = last(i, i2, j)
                if i == 0 and j == 0:
                    me = jnp.logical_and(aligned, g == 0)

                    @pl.when(me)
                    def _():
                        pltpu.make_async_copy(src, fin.at[g, i, j], f_r.at[g, i, j]).start()

                    @pl.when(jnp.logical_not(me))
                    def _():
                        send(src, fin.at[g, i, j], f_s.at[i, i2, j], f_r.at[g, i, j], to).start()
                else:
                    send(src, fin.at[g, i, j], f_s.at[i, i2, j], f_r.at[g, i, j], to).start()

    for i in range(2):
        for j in range(2):
            for g in range(2):
                send(fin.at[g, i, j], fin.at[g, i, j], f_s.at[0, 0, 0], f_r.at[g, i, j], sib).wait_recv()
            t = fin[0, i, j].astype(jnp.float32) + fin[1, i, j].astype(jnp.float32)
            gh[:, pl.ds(pl.multiple_of(xor(z0, i) * 512 + xor(c, j) * 256, 256), 256)] = t.astype(jnp.bfloat16)

    for cp in gc:
        cp.wait_recv()
    t = own[...]
    for r in range(3):
        t = t + grecv[r].astype(jnp.float32)
    gw[0] = t.astype(jnp.bfloat16)

    for cp in hz + wc + hc + hx + gc:
        cp.wait_send()
    for kk in (1, 2, 3):
        kz[kk].wait_send()
    for kk in range(4):
        kf[kk].wait_send()
    for kk in range(4):
        for r in range(4):
            qq = xor(2 * xor(y0, r % 2) + xor(z1, kk // 2), x)

            @pl.when(qq != 0)
            def _():
                send(st.at[kk, r], st.at[kk, r], x_s.at[kk, r], x_r.at[0, 0, 0], sib).wait_send()
    for i in range(2):
        for i2 in range(2):
            for j in range(2):
                cp = send(fs.at[i, i2, pl.ds(j * TOK, TOK)], fin.at[0, 0, 0], f_s.at[i, i2, j], f_r.at[0, 0, 0], sib)
                if i == 0 and j == 0:
                    me = jnp.logical_and(aligned, xor(y1, i2) == h)

                    @pl.when(jnp.logical_not(me))
                    def _():
                        cp.wait_send()
                else:
                    cp.wait_send()


def local(hidden, w_kv, queries, keys, values, out_grad, doc_lengths):
    bf, f32, dma = jnp.bfloat16, jnp.float32, pltpu.SemaphoreType.DMA
    vm, hbm = pl.BlockSpec(memory_space=pltpu.VMEM), pl.BlockSpec(memory_space=pl.ANY)
    return pl.pallas_call(
        body,
        out_shape=(jax.ShapeDtypeStruct((TOK, 1024), bf), jax.ShapeDtypeStruct((1, 256, KV2), bf)),
        in_specs=[pl.BlockSpec(memory_space=pltpu.SMEM), hbm, hbm, vm, vm, vm, vm],
        out_specs=(vm, vm),
        scratch_shapes=[
            pltpu.VMEM((4, 1024, 256), bf),
            pltpu.VMEM((4, 256, 1024), bf),
            pltpu.VMEM((4, 256, KV2), bf),
            pltpu.VMEM((1024, KV2), bf),
            pltpu.VMEM((4, 4, 256, 256), bf),
            pltpu.VMEM((4, 2, 2, 256, 256), bf),
            pltpu.VMEM((256, KV2), f32),
            pltpu.VMEM((3, 256, KV2), bf),
            pltpu.VMEM((3, 256, KV2), bf),
            pltpu.VMEM((2, 2, 256, 256), bf),
            pltpu.VMEM((2, 2, 2, TOK, 256), bf),
            dma((4, 2)), dma((4, 2)), dma((4,)), dma((4,)), dma((4,)), dma((4,)), dma((4,)), dma((4,)),
            dma((4,)), dma((4,)), dma((4,)), dma((4,)),
            dma((4, 4)), dma((4, 2, 2)), dma((4,)), dma((4,)), dma((2, 2, 2)), dma((2, 2, 2)), dma((5,)),
        ],
        compiler_params=pltpu.CompilerParams(
            collective_id=0, has_side_effects=True, vmem_limit_bytes=48 * 2**20),
        cost_estimate=pl.CostEstimate(flops=5 * 10**9, bytes_accessed=8 * 2**20, transcendentals=2**19),
    )(doc_lengths, hidden, w_kv, queries, keys, values, out_grad)


def solution(mesh):
    return jax.shard_map(
        local,
        mesh=mesh,
        in_specs=(
            P("dp", None),
            P("layer", "dp", None),
            P("layer", "dp", None),
            P("layer", "dp", None),
            P("layer", "dp", None),
            P("layer", "dp", None),
            P("dp", None),
        ),
        out_specs=(P("dp", "layer"), P("layer", "dp", None)),
        check_vma=False,
    )
```

```python
import jax
import jax.numpy as jnp
from jax import lax
from jax.experimental import pallas as pl
from jax.experimental.pallas import tpu as pltpu
from jax.sharding import PartitionSpec as P

HEAD = 128
GROUPS = 4
PER = 8
TOK = 128
DOCS = 8
KV = 512
KV2 = 1024
SCALE = HEAD ** (-0.5)
MESH = pl.DeviceIdType.MESH
NT = (((1,), (1,)), ((), ()))
HALF = (pl.ds(0, 128), pl.ds(128, 128))
PART = (pl.ds(256, 384), pl.ds(640, 384))


def xor(a, b):
    return jnp.bitwise_xor(a, b)


def body(lens_in, hidden, w, q_in, k_in, v_in, dout_in, gh, gw,
         lens, q, k, v, dout,
         hsrc, hid, hid_t, wb, kvb, st, rs, own, keep, gs2, gr2, gsend, grecv, fs, fin,
         hz_s, hz_r, hc_s, hc_r, hx_s, hx_r, w_s, w_r, kz_s, kz_r, kf_s, kf_r,
         x_s, x_r, g_s, g_r, g2_s, g2_r, f_s, f_r, loc):
    dp, ly = lax.axis_index("dp"), lax.axis_index("layer")
    y, z, c = dp // 8, lax.rem(dp // 2, 4), lax.rem(dp, 2)
    h, x = ly // 4, lax.rem(ly, 4)
    y0, y1, z0, z1, x0, x1 = lax.rem(y, 2), y // 2, lax.rem(z, 2), z // 2, lax.rem(x, 2), x // 2

    def dev(yy, zz, cc, hh, xx):
        return ((yy * 4 + zz) * 2 + cc, hh * 4 + xx)

    def ring(d, cc):
        p = lax.rem(h * 4 + z + d + 8, 8)
        return dev(y, lax.rem(p, 4), cc, p // 4, x)

    def send(src, dst, s, r, to):
        return pltpu.make_async_remote_copy(src_ref=src, dst_ref=dst, send_sem=s, recv_sem=r,
                                            device_id=to, device_id_type=MESH)

    def signal(to):
        pl.semaphore_signal(barrier, inc=1, device_id=to, device_id_type=MESH)

    ta, tb = xor(x1, y0), xor(x0, z1)
    aligned = tb == 0
    middle = z0 != z1
    xt = 2 * x1 + z1

    def last(i, i2, j):
        return dev(y, 2 * x0 + xor(z0, i), xor(c, j), xor(y1, i2), xt)

    sib = dev(y, z, 1 - c, h, x)
    zdev = {kk: dev(y, xor(z, kk), c, h, x) for kk in (1, 3)}
    xdev = {qq: dev(y, z, c, h, xor(x, qq)) for qq in (1, 2, 3)}
    ydev = {r: dev(xor(y, r), z, c, h, x) for r in (1, 3)}

    barrier = pltpu.get_barrier_semaphore()
    for to in [sib, zdev[1], xdev[1], xdev[2], xdev[3], ydev[1], ydev[3],
               ring(1, 0), ring(1, 1), ring(-1, 0), ring(-1, 1), ring(-2, 0), ring(2, 1)]:
        signal(to)

    @pl.when(middle)
    def _():
        signal(zdev[3])

    for i in range(2):
        for i2 in range(2):
            for j in range(2):
                to = last(i, i2, j)
                if i == 0 and j == 0:
                    @pl.when(jnp.logical_not(jnp.logical_and(aligned, xor(y1, i2) == h)))
                    def _():
                        signal(to)
                else:
                    signal(to)

    def columns(p, zz, cc):
        return pl.ds(pl.multiple_of(p * 2048 + zz * 512 + cc * 256, 256), 256)

    loads = [pltpu.make_async_copy(lens_in, lens, loc.at[0])]
    for n, (src, dst) in enumerate(((k_in, k), (q_in, q), (v_in, v), (dout_in, dout))):
        loads.append(pltpu.make_async_copy(src.at[0], dst, loc.at[1 + n]))
    for r in range(4):
        loads.append(pltpu.make_async_copy(hidden.at[:, columns(xor(y, r), z, c)],
                                           hid.at[r, pl.ds(0, TOK)], loc.at[5 + r]))
    loads.append(pltpu.make_async_copy(w.at[0], wb.at[0], loc.at[9]))
    steps = (1, -1, 2 - 4 * c)
    first = [pltpu.make_async_copy(hidden.at[:, columns(xor(y, x), lax.rem(z + d + 4, 4), xor(c, j))],
                                   hsrc.at[n, j], loc.at[10 + 2 * n + j])
             for n, d in enumerate(steps) for j in range(2)]
    for cp in first + loads[9:] + loads[:9]:
        cp.start()
    for cp in first + loads[9:]:
        cp.wait()

    pl.semaphore_wait(barrier, 20 + jnp.where(middle, 1, 0) + jnp.where(aligned, 0, 1))

    hz = []
    for n, d in enumerate(steps):
        zt = lax.rem(z + d + 4, 4)
        for j in range(2):
            cc = xor(c, j)
            rows = pl.ds(pl.multiple_of(xor(z, zt) * 256 + j * TOK, TOK), TOK)
            hz.append(send(hsrc.at[n, j], hid.at[x, rows], hz_s.at[n, j], hz_r.at[n, j], ring(d, cc)))
    wc = {(r, n): send(wb.at[0, HALF[n]], wb.at[r, HALF[n]], w_s.at[r - 1, n], w_r.at[r - 1, n], ydev[r])
          for r, n in ((1, 0), (3, 1), (1, 1), (3, 0))}
    wc[2, 0] = send(wb.at[1, HALF[0]], wb.at[2, HALF[0]], w_s.at[1, 0], w_r.at[1, 0], ydev[3])
    wc[2, 1] = send(wb.at[3, HALF[1]], wb.at[2, HALF[1]], w_s.at[1, 1], w_r.at[1, 1], ydev[1])
    hc = [send(hidden.at[:, columns(xor(y, r), z, 1 - c)], hid.at[r, pl.ds(TOK, TOK)],
               hc_s.at[r], hc_r.at[r], sib) for r in range(4)]
    for cp in hz:
        cp.start()
    for key in ((1, 0), (3, 1)):
        wc[key].start()
    for cp in hc:
        cp.start()

    loads[0].wait()
    row = lax.broadcasted_iota(jnp.int32, (TOK, TOK), 0)
    col = lax.broadcasted_iota(jnp.int32, (TOK, TOK), 1)
    doc_row, doc_col = jnp.zeros_like(row), jnp.zeros_like(col)
    end = jnp.int32(0)
    for d in range(DOCS):
        end = end + lens[0, d]
        doc_row = doc_row + jnp.where(row >= end, 1, 0)
        doc_col = doc_col + jnp.where(col >= end, 1, 0)
    bias = jnp.where((doc_row == doc_col) & (row <= col), 0.0, 1.0)
    off = jnp.concatenate([bias] * PER, axis=1) > 0.5
    for cp in loads[1:5]:
        cp.wait()

    def group(g, _):
        wide = pl.multiple_of(g * PER * HEAD, PER * HEAD)
        narrow = pl.multiple_of(g * HEAD, HEAD)
        qg, og = q[:, pl.ds(wide, PER * HEAD)], dout[:, pl.ds(wide, PER * HEAD)]
        qs = jnp.concatenate([qg[:, n * HEAD:(n + 1) * HEAD] for n in range(PER)], axis=0)
        os = jnp.concatenate([og[:, n * HEAD:(n + 1) * HEAD] for n in range(PER)], axis=0)
        kg, vg = k[:, pl.ds(narrow, HEAD)], v[:, pl.ds(narrow, HEAD)]
        s = lax.dot_general(kg, qs, NT, preferred_element_type=jnp.float32) * SCALE
        s = jnp.where(off, jnp.float32(-1e30), s)
        e = jnp.exp(s - jnp.max(s, axis=0, keepdims=True))
        p = e / jnp.sum(e, axis=0, keepdims=True)
        pb = p.astype(jnp.bfloat16)
        dp_ = lax.dot_general(vg, os, NT, preferred_element_type=jnp.float32)
        delta = jnp.sum(pb.astype(jnp.float32) * dp_, axis=0, keepdims=True)
        ds = (p * (dp_ - delta)).astype(jnp.bfloat16)
        dv = jnp.dot(pb, os, preferred_element_type=jnp.float32)
        dk = jnp.dot(ds, qs, preferred_element_type=jnp.float32) * SCALE
        kvb[0:TOK, pl.ds(narrow, HEAD)] = dk.astype(jnp.bfloat16)
        kvb[0:TOK, pl.ds(pl.multiple_of(KV + g * HEAD, HEAD), HEAD)] = dv.astype(jnp.bfloat16)
        return 0

    lax.fori_loop(0, GROUPS, group, 0)

    def kv_rows(kk, j):
        return pl.ds(kk * 256 + j * TOK, TOK)

    def kv_send(src, to, dst, n):
        return send(kvb.at[kv_rows(src, 0)], kvb.at[kv_rows(dst, 0)], kz_s.at[n], kz_r.at[dst], zdev[to])

    kz = {1: kv_send(0, 1, 1, 0), 3: kv_send(0, 3, 3, 1), 2: kv_send(3, 1, 2, 2)}
    kp = {1: kv_send(1, 3, 2, 3), 3: kz[2], 2: kv_send(2, 1, 3, 4)}
    kf = {kk: send(kvb.at[kv_rows(kk, 0)], kvb.at[kv_rows(kk, 1)], kf_s.at[kk], kf_r.at[kk], sib)
          for kk in range(4)}
    kz[1].start()

    @pl.when(middle)
    def _():
        kz[3].start()

    kf[0].start()
    for key in ((1, 1), (3, 0)):
        wc[key].start()

    for cp in hz:
        cp.wait_recv()
    hx = {(qq, n): send(hid.at[x, PART[n]], hid.at[x, PART[n]], hx_s.at[qq - 1, n], hx_r.at[qq - 1, n], xdev[qq])
          for qq, n in ((1, 0), (3, 1), (1, 1), (3, 0))}
    hx[2, 0] = send(hid.at[xor(x, 1), PART[0]], hid.at[xor(x, 1), PART[0]], hx_s.at[1, 0], hx_r.at[1, 0], xdev[3])
    hx[2, 1] = send(hid.at[xor(x, 3), PART[1]], hid.at[xor(x, 3), PART[1]], hx_s.at[1, 1], hx_r.at[1, 1], xdev[1])
    for key in ((1, 0), (3, 1)):
        hx[key].start()

    def tile(kk, r):
        t = lax.dot_general(kvb[kk * 256:(kk + 1) * 256], wb[r], NT, preferred_element_type=jnp.float32)
        st[kk, r] = t.astype(jnp.bfloat16)
        b, i, a, i2 = kk // 2, kk % 2, r % 2, r // 2
        qq = 2 * xor(ta, a) + xor(tb, b)

        @pl.when(qq != 0)
        def _():
            send(st.at[kk, r], rs.at[qq - 1, i, i2], x_s.at[qq - 1, i, i2], x_r.at[qq - 1, i, i2],
                 dev(y, z, c, h, xor(x, qq))).start()

    def finish(b, i):
        @pl.when(tb == b)
        def _():
            for i2 in range(2):
                finish_tile(i, i2)

    def finish_tile(i, i2):
        for n in range(3):
            send(rs.at[n, i, i2], rs.at[n, i, i2], x_s.at[n, i, i2], x_r.at[n, i, i2], sib).wait_recv()
        t = st[2 * tb + i, ta + 2 * i2].astype(jnp.float32)
        for n in range(3):
            t = t + rs[n, i, i2].astype(jnp.float32)
        fs[i, i2] = t.astype(jnp.bfloat16)
        g = xor(xor(y1, i2), h)
        for j in range(2):
            src = fs.at[i, i2, pl.ds(j * TOK, TOK)]
            to = last(i, i2, j)
            if i == 0 and j == 0:
                me = jnp.logical_and(aligned, g == 0)

                @pl.when(me)
                def _():
                    pltpu.make_async_copy(src, fin.at[g, i, j], f_r.at[g, i, j]).start()

                @pl.when(jnp.logical_not(me))
                def _():
                    send(src, fin.at[g, i, j], f_s.at[i, i2, j], f_r.at[g, i, j], to).start()
            else:
                send(src, fin.at[g, i, j], f_s.at[i, i2, j], f_r.at[g, i, j], to).start()

    wc[1, 0].wait_recv()
    wc[2, 0].start()
    wc[3, 1].wait_recv()
    wc[2, 1].start()
    for key in ((1, 1), (3, 0)):
        hx[key].start()
    kf[0].wait_recv()
    tile(0, 0)
    kz[1].wait_recv()

    @pl.when(middle)
    def _():
        kp[1].start()
        kz[3].wait_recv()
        kp[3].start()
        kf[3].start()

    kf[1].start()
    for key, nxt in (((1, 0), (2, 0)), ((3, 1), (2, 1))):
        hx[key].wait_recv()
        hx[nxt].start()
    for r, n in ((1, 1), (3, 0)):
        wc[r, n].wait_recv()
        tile(0, r)
    kf[1].wait_recv()
    for r in (0, 1, 3):
        tile(1, r)
    kz[2].wait_recv()

    @pl.when(middle)
    def _():
        kp[2].start()

    kf[2].start()
    for n in range(2):
        wc[2, n].wait_recv()
    tile(0, 2)
    tile(1, 2)
    kf[2].wait_recv()
    for r in (2, 1, 3, 0):
        tile(2, r)

    @pl.when(jnp.logical_not(middle))
    def _():
        kz[3].wait_recv()
        kf[3].start()

    kf[3].wait_recv()
    for r in (2, 1, 3, 0):
        tile(3, r)
    for key in ((1, 1), (3, 0), (2, 0), (2, 1)):
        hx[key].wait_recv()
    for cp in hc:
        cp.wait_recv()
    for cp in loads[5:9]:
        cp.wait()
    for r in range(4):
        hid_t[r] = hid[r].T

    def weight(r):
        return jnp.dot(hid_t[r], kvb[...], preferred_element_type=jnp.float32)

    g2 = [send(gs2.at[HALF[n]], gr2.at[n], g2_s.at[n], g2_r.at[n], ydev[3 if n else 1]) for n in range(2)]
    gc = {(r, n): send(gsend.at[r // 2, HALF[n]], grecv.at[r // 2, HALF[n]], g_s.at[r // 2, n], g_r.at[r // 2, n],
                       ydev[r]) for r in (1, 3) for n in range(2)}
    gs2[...] = weight(2).astype(jnp.bfloat16)
    for cp in g2:
        cp.start()
    t = weight(1)
    gsend[0, 0:128] = t[0:128].astype(jnp.bfloat16)
    keep[0] = t[128:256]
    gc[1, 0].start()
    t = weight(3)
    gsend[1, 128:256] = t[128:256].astype(jnp.bfloat16)
    keep[1] = t[0:128]
    gc[3, 1].start()
    finish(0, 0)
    finish(0, 1)
    finish(1, 0)
    own[...] = weight(0)
    g2[0].wait_recv()
    gsend[1, 0:128] = (keep[1] + gr2[0].astype(jnp.float32)).astype(jnp.bfloat16)
    gc[3, 0].start()
    g2[1].wait_recv()
    gsend[0, 128:256] = (keep[0] + gr2[1].astype(jnp.float32)).astype(jnp.bfloat16)
    gc[1, 1].start()

    finish(1, 1)
    for i in range(2):
        for j in range(2):
            for g in range(2):
                send(fin.at[g, i, j], fin.at[g, i, j], f_s.at[0, 0, 0], f_r.at[g, i, j], sib).wait_recv()
            t = fin[0, i, j].astype(jnp.float32) + fin[1, i, j].astype(jnp.float32)
            gh[:, pl.ds(pl.multiple_of(xor(z0, i) * 512 + xor(c, j) * 256, 256), 256)] = t.astype(jnp.bfloat16)

    for cp in gc.values():
        cp.wait_recv()
    gw[0] = (own[...] + grecv[0].astype(jnp.float32) + grecv[1].astype(jnp.float32)).astype(jnp.bfloat16)

    for cp in hz + hc + g2 + list(wc.values()) + list(hx.values()) + list(gc.values()):
        cp.wait_send()
    kz[1].wait_send()

    @pl.when(middle)
    def _():
        kz[3].wait_send()
        for kk in (1, 2, 3):
            kp[kk].wait_send()

    for kk in range(4):
        kf[kk].wait_send()
    for i in range(2):
        for i2 in range(2):
            for n in range(3):
                send(rs.at[n, i, i2], rs.at[n, i, i2], x_s.at[n, i, i2], x_r.at[n, i, i2], sib).wait_send()
            for j in range(2):
                cp = send(fs.at[i, i2, pl.ds(j * TOK, TOK)], fin.at[0, 0, 0], f_s.at[i, i2, j], f_r.at[0, 0, 0], sib)
                if i == 0 and j == 0:
                    @pl.when(jnp.logical_not(jnp.logical_and(aligned, xor(y1, i2) == h)))
                    def _():
                        cp.wait_send()
                else:
                    cp.wait_send()


def local(hidden, w_kv, queries, keys, values, out_grad, doc_lengths):
    bf, f32, dma = jnp.bfloat16, jnp.float32, pltpu.SemaphoreType.DMA
    vm, hbm = pl.BlockSpec(memory_space=pltpu.VMEM), pl.BlockSpec(memory_space=pltpu.HBM)
    return pl.pallas_call(
        body,
        out_shape=(jax.ShapeDtypeStruct((TOK, 1024), bf), jax.ShapeDtypeStruct((1, 256, KV2), bf)),
        in_specs=[hbm] * 7,
        out_specs=(vm, vm),
        scratch_shapes=[
            pltpu.SMEM((1, DOCS), jnp.int32),
            pltpu.VMEM((TOK, 4096), bf),
            pltpu.VMEM((TOK, KV), bf),
            pltpu.VMEM((TOK, KV), bf),
            pltpu.VMEM((TOK, 4096), bf),
            pltpu.VMEM((3, 2, TOK, 256), bf),
            pltpu.VMEM((4, 1024, 256), bf),
            pltpu.VMEM((4, 256, 1024), bf),
            pltpu.VMEM((4, 256, KV2), bf),
            pltpu.VMEM((1024, KV2), bf),
            pltpu.VMEM((4, 4, 256, 256), bf),
            pltpu.VMEM((3, 2, 2, 256, 256), bf),
            pltpu.VMEM((256, KV2), f32),
            pltpu.VMEM((2, 128, KV2), f32),
            pltpu.VMEM((256, KV2), bf),
            pltpu.VMEM((2, 128, KV2), bf),
            pltpu.VMEM((2, 256, KV2), bf),
            pltpu.VMEM((2, 256, KV2), bf),
            pltpu.VMEM((2, 2, 256, 256), bf),
            pltpu.VMEM((2, 2, 2, TOK, 256), bf),
            dma((3, 2)), dma((3, 2)), dma((4,)), dma((4,)), dma((3, 2)), dma((3, 2)), dma((3, 2)), dma((3, 2)),
            dma((5,)), dma((4,)), dma((4,)), dma((4,)),
            dma((3, 2, 2)), dma((3, 2, 2)),
            dma((2, 2)), dma((2, 2)), dma((2,)), dma((2,)), dma((2, 2, 2)), dma((2, 2, 2)), dma((16,)),
        ],
        compiler_params=pltpu.CompilerParams(
            collective_id=0, has_side_effects=True, vmem_limit_bytes=60 * 2**20),
        cost_estimate=pl.CostEstimate(flops=5 * 10**9, bytes_accessed=8 * 2**20, transcendentals=2**19),
    )(doc_lengths, hidden, w_kv, queries, keys, values, out_grad)


def solution(mesh):
    return jax.shard_map(
        local,
        mesh=mesh,
        in_specs=(
            P("dp", None),
            P("layer", "dp", None),
            P("layer", "dp", None),
            P("layer", "dp", None),
            P("layer", "dp", None),
            P("layer", "dp", None),
            P("dp", None),
        ),
        out_specs=(P("dp", "layer"), P("layer", "dp", None)),
        check_vma=False,
    )
```

```python
import jax
import jax.numpy as jnp
from jax import lax
from jax.experimental import pallas as pl
from jax.experimental.pallas import tpu as pltpu
from jax.sharding import PartitionSpec as P

HEAD = 128
GROUPS = 4
PER = 8
TOK = 128
DOCS = 8
KV = 512
KV2 = 1024
SCALE = HEAD ** (-0.5)
MESH = pl.DeviceIdType.MESH
NT = (((1,), (1,)), ((), ()))
HALF = (pl.ds(0, 128), pl.ds(128, 128))
PART = (pl.ds(256, 384), pl.ds(640, 384))


def xor(a, b):
    return jnp.bitwise_xor(a, b)


def body(lens_in, hidden, w, q_in, k_in, v_in, dout_in, gh, gw,
         lens, q, k, v, dout,
         hsrc, hid, hid_t, wb, kvb, st, rs, own, keep, gs2, gr2, gsend, grecv, fs, fin,
         hz_s, hz_r, hc_s, hc_r, hx_s, hx_r, w_s, w_r, kz_s, kz_r, kf_s, kf_r,
         x_s, x_r, g_s, g_r, g2_s, g2_r, f_s, f_r, loc):
    dp, ly = lax.axis_index("dp"), lax.axis_index("layer")
    y, z, c = dp // 8, lax.rem(dp // 2, 4), lax.rem(dp, 2)
    h, x = ly // 4, lax.rem(ly, 4)
    y0, y1, z0, z1, x0, x1 = lax.rem(y, 2), y // 2, lax.rem(z, 2), z // 2, lax.rem(x, 2), x // 2

    def dev(yy, zz, cc, hh, xx):
        return ((yy * 4 + zz) * 2 + cc, hh * 4 + xx)

    def ring(d, cc):
        p = lax.rem(h * 4 + z + d + 8, 8)
        return dev(y, lax.rem(p, 4), cc, p // 4, x)

    def send(src, dst, s, r, to):
        return pltpu.make_async_remote_copy(src_ref=src, dst_ref=dst, send_sem=s, recv_sem=r,
                                            device_id=to, device_id_type=MESH)

    def signal(to):
        pl.semaphore_signal(barrier, inc=1, device_id=to, device_id_type=MESH)

    ta, tb = xor(x1, y0), xor(x0, z1)
    aligned = tb == 0
    middle = z0 != z1
    xt = 2 * x1 + z1

    def last(i, i2, j):
        return dev(y, 2 * x0 + xor(z0, i), xor(c, j), xor(y1, i2), xt)

    sib = dev(y, z, 1 - c, h, x)
    zdev = {kk: dev(y, xor(z, kk), c, h, x) for kk in (1, 3)}
    xdev = {qq: dev(y, z, c, h, xor(x, qq)) for qq in (1, 2, 3)}
    ydev = {r: dev(xor(y, r), z, c, h, x) for r in (1, 3)}

    barrier = pltpu.get_barrier_semaphore()
    for to in [sib, zdev[1], xdev[1], xdev[2], xdev[3], ydev[1], ydev[3],
               ring(1, 0), ring(1, 1), ring(-1, 0), ring(-1, 1), ring(-2, 0), ring(2, 1)]:
        signal(to)

    @pl.when(middle)
    def _():
        signal(zdev[3])

    for i in range(2):
        for i2 in range(2):
            for j in range(2):
                to = last(i, i2, j)
                if i == 0 and j == 0:
                    @pl.when(jnp.logical_not(jnp.logical_and(aligned, xor(y1, i2) == h)))
                    def _():
                        signal(to)
                else:
                    signal(to)

    def columns(p, zz, cc):
        return pl.ds(pl.multiple_of(p * 2048 + zz * 512 + cc * 256, 256), 256)

    loads = [pltpu.make_async_copy(lens_in, lens, loc.at[0])]
    for n, (src, dst) in enumerate(((k_in, k), (q_in, q), (v_in, v), (dout_in, dout))):
        loads.append(pltpu.make_async_copy(src.at[0], dst, loc.at[1 + n]))
    for r in range(4):
        loads.append(pltpu.make_async_copy(hidden.at[:, columns(xor(y, r), z, c)],
                                           hid.at[r, pl.ds(0, TOK)], loc.at[5 + r]))
    loads.append(pltpu.make_async_copy(w.at[0], wb.at[0], loc.at[9]))
    steps = (1, -1, 2 - 4 * c)
    first = [pltpu.make_async_copy(hidden.at[:, columns(xor(y, x), lax.rem(z + d + 4, 4), xor(c, j))],
                                   hsrc.at[n, j], loc.at[10 + 2 * n + j])
             for n, d in enumerate(steps) for j in range(2)]
    for cp in first + loads[9:] + loads[:9]:
        cp.start()
    for cp in first + loads[9:]:
        cp.wait()

    pl.semaphore_wait(barrier, 20 + jnp.where(middle, 1, 0) + jnp.where(aligned, 0, 1))

    hz = []
    for n, d in enumerate(steps):
        zt = lax.rem(z + d + 4, 4)
        for j in range(2):
            cc = xor(c, j)
            rows = pl.ds(pl.multiple_of(xor(z, zt) * 256 + j * TOK, TOK), TOK)
            hz.append(send(hsrc.at[n, j], hid.at[x, rows], hz_s.at[n, j], hz_r.at[n, j], ring(d, cc)))
    wc = {(r, n): send(wb.at[0, HALF[n]], wb.at[r, HALF[n]], w_s.at[r - 1, n], w_r.at[r - 1, n], ydev[r])
          for r, n in ((1, 0), (3, 1), (1, 1), (3, 0))}
    wc[2, 0] = send(wb.at[1, HALF[0]], wb.at[2, HALF[0]], w_s.at[1, 0], w_r.at[1, 0], ydev[3])
    wc[2, 1] = send(wb.at[3, HALF[1]], wb.at[2, HALF[1]], w_s.at[1, 1], w_r.at[1, 1], ydev[1])
    hc = [send(hidden.at[:, columns(xor(y, r), z, 1 - c)], hid.at[r, pl.ds(TOK, TOK)],
               hc_s.at[r], hc_r.at[r], sib) for r in range(4)]
    for cp in hz:
        cp.start()
    for key in ((1, 0), (3, 1)):
        wc[key].start()
    for cp in hc:
        cp.start()

    loads[0].wait()
    row = lax.broadcasted_iota(jnp.int32, (TOK, TOK), 0)
    col = lax.broadcasted_iota(jnp.int32, (TOK, TOK), 1)
    doc_row, doc_col = jnp.zeros_like(row), jnp.zeros_like(col)
    end = jnp.int32(0)
    for d in range(DOCS):
        end = end + lens[0, d]
        doc_row = doc_row + jnp.where(row >= end, 1, 0)
        doc_col = doc_col + jnp.where(col >= end, 1, 0)
    bias = jnp.where((doc_row == doc_col) & (row <= col), 0.0, 1.0)
    off = jnp.concatenate([bias] * PER, axis=1) > 0.5
    for cp in loads[1:5]:
        cp.wait()

    def group(g, _):
        wide = pl.multiple_of(g * PER * HEAD, PER * HEAD)
        narrow = pl.multiple_of(g * HEAD, HEAD)
        qg, og = q[:, pl.ds(wide, PER * HEAD)], dout[:, pl.ds(wide, PER * HEAD)]
        qs = jnp.concatenate([qg[:, n * HEAD:(n + 1) * HEAD] for n in range(PER)], axis=0)
        os = jnp.concatenate([og[:, n * HEAD:(n + 1) * HEAD] for n in range(PER)], axis=0)
        kg, vg = k[:, pl.ds(narrow, HEAD)], v[:, pl.ds(narrow, HEAD)]
        s = lax.dot_general(kg, qs, NT, preferred_element_type=jnp.float32) * SCALE
        s = jnp.where(off, jnp.float32(-1e30), s)
        e = jnp.exp(s - jnp.max(s, axis=0, keepdims=True))
        p = e / jnp.sum(e, axis=0, keepdims=True)
        pb = p.astype(jnp.bfloat16)
        dp_ = lax.dot_general(vg, os, NT, preferred_element_type=jnp.float32)
        delta = jnp.sum(pb.astype(jnp.float32) * dp_, axis=0, keepdims=True)
        ds = (p * (dp_ - delta)).astype(jnp.bfloat16)
        dv = jnp.dot(pb, os, preferred_element_type=jnp.float32)
        dk = jnp.dot(ds, qs, preferred_element_type=jnp.float32) * SCALE
        kvb[0:TOK, pl.ds(narrow, HEAD)] = dk.astype(jnp.bfloat16)
        kvb[0:TOK, pl.ds(pl.multiple_of(KV + g * HEAD, HEAD), HEAD)] = dv.astype(jnp.bfloat16)
        return 0

    lax.fori_loop(0, GROUPS, group, 0)

    def kv_rows(kk, j):
        return pl.ds(kk * 256 + j * TOK, TOK)

    def kv_send(src, to, dst, n):
        return [send(kvb.at[pl.ds(src * 256 + m * 64, 64)], kvb.at[pl.ds(dst * 256 + m * 64, 64)],
                     kz_s.at[n, m], kz_r.at[dst, m], zdev[to]) for m in range(2)]

    kz = {1: kv_send(0, 1, 1, 0), 3: kv_send(0, 3, 3, 1), 2: kv_send(3, 1, 2, 2)}
    kp = {1: kv_send(1, 3, 2, 3), 3: kz[2], 2: kv_send(2, 1, 3, 4)}
    kf = {kk: send(kvb.at[kv_rows(kk, 0)], kvb.at[kv_rows(kk, 1)], kf_s.at[kk], kf_r.at[kk], sib)
          for kk in range(4)}
    for m in range(2):
        kz[1][m].start()

        @pl.when(middle)
        def _():
            kz[3][m].start()

    kf[0].start()
    for key in ((1, 1), (3, 0)):
        wc[key].start()
    hx = {(qq, n): send(hid.at[x, PART[n]], hid.at[x, PART[n]], hx_s.at[qq - 1, n], hx_r.at[qq - 1, n], xdev[qq])
          for qq, n in ((1, 0), (3, 1), (1, 1), (3, 0))}
    hx[2, 0] = send(hid.at[xor(x, 1), PART[0]], hid.at[xor(x, 1), PART[0]], hx_s.at[1, 0], hx_r.at[1, 0], xdev[3])
    hx[2, 1] = send(hid.at[xor(x, 3), PART[1]], hid.at[xor(x, 3), PART[1]], hx_s.at[1, 1], hx_r.at[1, 1], xdev[1])

    def tile(kk, r):
        t = lax.dot_general(kvb[kk * 256:(kk + 1) * 256], wb[r], NT, preferred_element_type=jnp.float32)
        st[kk, r] = t.astype(jnp.bfloat16)
        b, i, a, i2 = kk // 2, kk % 2, r % 2, r // 2
        qq = 2 * xor(ta, a) + xor(tb, b)

        @pl.when(qq != 0)
        def _():
            send(st.at[kk, r], rs.at[qq - 1, i, i2], x_s.at[qq - 1, i, i2], x_r.at[qq - 1, i, i2],
                 dev(y, z, c, h, xor(x, qq))).start()

    def finish(b, i):
        @pl.when(tb == b)
        def _():
            for far in (1, 0):
                finish_tile(i, xor(xor(y1, h), far))

    def finish_tile(i, i2):
        for n in range(3):
            send(rs.at[n, i, i2], rs.at[n, i, i2], x_s.at[n, i, i2], x_r.at[n, i, i2], sib).wait_recv()
        t = st[2 * tb + i, ta + 2 * i2].astype(jnp.float32)
        for n in range(3):
            t = t + rs[n, i, i2].astype(jnp.float32)
        fs[i, i2] = t.astype(jnp.bfloat16)
        g = xor(xor(y1, i2), h)
        for j in range(2):
            src = fs.at[i, i2, pl.ds(j * TOK, TOK)]
            to = last(i, i2, j)
            if i == 0 and j == 0:
                me = jnp.logical_and(aligned, g == 0)

                @pl.when(me)
                def _():
                    pltpu.make_async_copy(src, fin.at[g, i, j], f_r.at[g, i, j]).start()

                @pl.when(jnp.logical_not(me))
                def _():
                    send(src, fin.at[g, i, j], f_s.at[i, i2, j], f_r.at[g, i, j], to).start()
            else:
                send(src, fin.at[g, i, j], f_s.at[i, i2, j], f_r.at[g, i, j], to).start()

    def hidden_on(keys):
        for key in keys:
            hx[key].start()

    def hidden_in():
        for cp in hz:
            cp.wait_recv()
        hidden_on(((1, 0), (3, 1)))

    def hidden_pass():
        for key, nxt in (((1, 0), (2, 0)), ((3, 1), (2, 1))):
            hx[key].wait_recv()
            hx[nxt].start()

    def kv_pass(m):
        @pl.when(middle)
        def _():
            for kk in (1, 3):
                kz[kk][m].wait_recv()
                kp[kk][m].start()

    hidden_in()
    hidden_on(((1, 1), (3, 0)))
    hidden_pass()
    wc[1, 0].wait_recv()
    wc[2, 0].start()
    wc[3, 1].wait_recv()
    wc[2, 1].start()
    kf[0].wait_recv()
    tile(0, 0)
    kv_pass(0)
    kv_pass(1)

    @pl.when(middle)
    def _():
        kf[3].start()

    @pl.when(jnp.logical_not(middle))
    def _():
        for m in range(2):
            kz[1][m].wait_recv()

    kf[1].start()
    for r, n in ((1, 1), (3, 0)):
        wc[r, n].wait_recv()
        tile(0, r)
    kf[1].wait_recv()
    for r in (0, 1, 3):
        tile(1, r)
    for m in range(2):
        kz[2][m].wait_recv()

        @pl.when(middle)
        def _():
            kp[2][m].start()

    kf[2].start()
    for n in range(2):
        wc[2, n].wait_recv()
    tile(0, 2)
    tile(1, 2)
    kf[2].wait_recv()
    for r in (2, 1, 3, 0):
        tile(2, r)

    @pl.when(jnp.logical_not(middle))
    def _():
        for m in range(2):
            kz[3][m].wait_recv()
        kf[3].start()

    kf[3].wait_recv()
    for r in (2, 1, 3, 0):
        tile(3, r)
    for key in ((1, 1), (3, 0), (2, 0), (2, 1)):
        hx[key].wait_recv()
    for cp in hc:
        cp.wait_recv()
    for cp in loads[5:9]:
        cp.wait()
    for r in range(4):
        hid_t[r] = hid[r].T

    def weight(r):
        return jnp.dot(hid_t[r], kvb[...], preferred_element_type=jnp.float32)

    g2 = [send(gs2.at[HALF[n]], gr2.at[n], g2_s.at[n], g2_r.at[n], ydev[3 if n else 1]) for n in range(2)]
    gc = {(r, n): send(gsend.at[r // 2, HALF[n]], grecv.at[r // 2, HALF[n]], g_s.at[r // 2, n], g_r.at[r // 2, n],
                       ydev[r]) for r in (1, 3) for n in range(2)}
    gs2[...] = weight(2).astype(jnp.bfloat16)
    for cp in g2:
        cp.start()
    t = weight(1)
    gsend[0, 0:128] = t[0:128].astype(jnp.bfloat16)
    keep[0] = t[128:256]
    gc[1, 0].start()
    t = weight(3)
    gsend[1, 128:256] = t[128:256].astype(jnp.bfloat16)
    keep[1] = t[0:128]
    gc[3, 1].start()
    finish(0, 0)
    finish(0, 1)
    finish(1, 0)
    own[...] = weight(0)
    g2[0].wait_recv()
    gsend[1, 0:128] = (keep[1] + gr2[0].astype(jnp.float32)).astype(jnp.bfloat16)
    gc[3, 0].start()
    g2[1].wait_recv()
    gsend[0, 128:256] = (keep[0] + gr2[1].astype(jnp.float32)).astype(jnp.bfloat16)
    gc[1, 1].start()

    finish(1, 1)
    for i in range(2):
        for j in range(2):
            for g in range(2):
                send(fin.at[g, i, j], fin.at[g, i, j], f_s.at[0, 0, 0], f_r.at[g, i, j], sib).wait_recv()
            t = fin[0, i, j].astype(jnp.float32) + fin[1, i, j].astype(jnp.float32)
            gh[:, pl.ds(pl.multiple_of(xor(z0, i) * 512 + xor(c, j) * 256, 256), 256)] = t.astype(jnp.bfloat16)

    for cp in gc.values():
        cp.wait_recv()
    gw[0] = (own[...] + grecv[0].astype(jnp.float32) + grecv[1].astype(jnp.float32)).astype(jnp.bfloat16)

    for cp in hz + hc + g2 + list(wc.values()) + list(hx.values()) + list(gc.values()):
        cp.wait_send()
    for m in range(2):
        kz[1][m].wait_send()

        @pl.when(middle)
        def _():
            kz[3][m].wait_send()
            for kk in (1, 2, 3):
                kp[kk][m].wait_send()

    for kk in range(4):
        kf[kk].wait_send()
    for i in range(2):
        for i2 in range(2):
            for n in range(3):
                send(rs.at[n, i, i2], rs.at[n, i, i2], x_s.at[n, i, i2], x_r.at[n, i, i2], sib).wait_send()
            for j in range(2):
                cp = send(fs.at[i, i2, pl.ds(j * TOK, TOK)], fin.at[0, 0, 0], f_s.at[i, i2, j], f_r.at[0, 0, 0], sib)
                if i == 0 and j == 0:
                    @pl.when(jnp.logical_not(jnp.logical_and(aligned, xor(y1, i2) == h)))
                    def _():
                        cp.wait_send()
                else:
                    cp.wait_send()


def local(hidden, w_kv, queries, keys, values, out_grad, doc_lengths):
    bf, f32, dma = jnp.bfloat16, jnp.float32, pltpu.SemaphoreType.DMA
    vm, hbm = pl.BlockSpec(memory_space=pltpu.VMEM), pl.BlockSpec(memory_space=pltpu.HBM)
    return pl.pallas_call(
        body,
        out_shape=(jax.ShapeDtypeStruct((TOK, 1024), bf), jax.ShapeDtypeStruct((1, 256, KV2), bf)),
        in_specs=[hbm] * 7,
        out_specs=(vm, vm),
        scratch_shapes=[
            pltpu.SMEM((1, DOCS), jnp.int32),
            pltpu.VMEM((TOK, 4096), bf),
            pltpu.VMEM((TOK, KV), bf),
            pltpu.VMEM((TOK, KV), bf),
            pltpu.VMEM((TOK, 4096), bf),
            pltpu.VMEM((3, 2, TOK, 256), bf),
            pltpu.VMEM((4, 1024, 256), bf),
            pltpu.VMEM((4, 256, 1024), bf),
            pltpu.VMEM((4, 256, KV2), bf),
            pltpu.VMEM((1024, KV2), bf),
            pltpu.VMEM((4, 4, 256, 256), bf),
            pltpu.VMEM((3, 2, 2, 256, 256), bf),
            pltpu.VMEM((256, KV2), f32),
            pltpu.VMEM((2, 128, KV2), f32),
            pltpu.VMEM((256, KV2), bf),
            pltpu.VMEM((2, 128, KV2), bf),
            pltpu.VMEM((2, 256, KV2), bf),
            pltpu.VMEM((2, 256, KV2), bf),
            pltpu.VMEM((2, 2, 256, 256), bf),
            pltpu.VMEM((2, 2, 2, TOK, 256), bf),
            dma((3, 2)), dma((3, 2)), dma((4,)), dma((4,)), dma((3, 2)), dma((3, 2)), dma((3, 2)), dma((3, 2)),
            dma((5, 2)), dma((4, 2)), dma((4,)), dma((4,)),
            dma((3, 2, 2)), dma((3, 2, 2)),
            dma((2, 2)), dma((2, 2)), dma((2,)), dma((2,)), dma((2, 2, 2)), dma((2, 2, 2)), dma((16,)),
        ],
        compiler_params=pltpu.CompilerParams(
            collective_id=0, has_side_effects=True, vmem_limit_bytes=60 * 2**20),
        cost_estimate=pl.CostEstimate(flops=5 * 10**9, bytes_accessed=8 * 2**20, transcendentals=2**19),
    )(doc_lengths, hidden, w_kv, queries, keys, values, out_grad)


def solution(mesh):
    return jax.shard_map(
        local,
        mesh=mesh,
        in_specs=(
            P("dp", None),
            P("layer", "dp", None),
            P("layer", "dp", None),
            P("layer", "dp", None),
            P("layer", "dp", None),
            P("layer", "dp", None),
            P("dp", None),
        ),
        out_specs=(P("dp", "layer"), P("layer", "dp", None)),
        check_vma=False,
    )
```
